512 devices in a mesh: grp: 16 (over x, y), dev: 32 (over z, core).
Axes of the slice: x: 4, y: 4, z: 16, core: 2. Of those that a mesh axis runs over, the one named last changes fastest.
Arguments:
- block_vectors: float32 [262144, 64], P(('grp', 'dev')), may hold values from -6 to 6
- hamiltonian: float32 [4096, 64, 2048], P(('grp', 'dev')), may hold values from -0.125 to 0.125
- pattern: int32 [4096, 32], P(('grp', 'dev')), may hold values from 0 to 4095, as said below
- owned_blocks: int32 [512], P(('grp', 'dev')), may hold values from 1 to 8, as said below
- spectrum: float32 [2], replicated, may hold values from 0.5 to 2
Outputs:
- basis: float32 [262144, 64], P(('grp', 'dev'))
- r_factor: float32 [64, 64], replicated
The draws below stay inside these ranges and needn't reach their ends.
Inputs may be any that keep to these rules, and one draw needn't show every extreme that they name: pattern[b, 0] = b; every other entry is b + o clipped to the slots, for a distinct nonzero o with |o| <= 16. `owned_blocks`: some device owns all 8 slots.
All inputs are finite; a program needn't handle non-finite values.
Results may differ from the reference program's by a relative error of at most 0.0003.
Values sent between devices are 32-bit elements; how exact they have to be, the bound alone decides.
A program may use at most 64 MiB of HBM per device.

```python
import math
import jax
import jax.numpy as jnp
from jax import lax

BS = 64
COLS = 64
NBR = 32
BAND = 16
RB_CAP = 8
NBLK = 4096
DEVICES = 512


def draw_pattern(key, part):
    key = jax.random.fold_in(key, 11)
    offsets_all = jnp.concatenate([jnp.arange(-BAND, 0, dtype=jnp.int32), jnp.arange(1, BAND + 1, dtype=jnp.int32)])
    row_keys = jax.random.split(key, NBLK)
    orders = jax.vmap(lambda single: jax.random.permutation(single, 2 * BAND))(row_keys)
    chosen = offsets_all[orders[:, :NBR - 1]]
    rows = jnp.arange(NBLK, dtype=jnp.int32)[:, None]
    others = jnp.clip(rows + chosen, 0, NBLK - 1)
    return jnp.concatenate([rows, others], axis=1).astype(jnp.int32)


def draw_owned_blocks(key, part):
    key = jax.random.fold_in(key, 23)
    key_base, key_full, key_pick = jax.random.split(key, 3)
    base = jax.random.randint(key_base, (DEVICES,), 1, max(1, RB_CAP // 2) + 1)
    full = jax.random.randint(key_full, (DEVICES,), 0, 8) == 0
    counts = jnp.where(full, RB_CAP, base)
    pick = jax.random.randint(key_pick, (), 0, DEVICES)
    counts = counts.at[pick].set(RB_CAP)
    return counts.astype(jnp.int32)


def block_levels(rng, shape, cuts, low, high):
    def one(dim, blocks):
        steps = jax.random.uniform(jax.random.fold_in(jax.random.fold_in(rng, 6), dim), (blocks,), jnp.float32, low / len(cuts), high / len(cuts))
        return jnp.repeat(jnp.exp(steps), shape[dim] // blocks).reshape((-1,) + (1,) * (len(shape) - dim - 1))

    gain = one(*cuts[0])
    for cut in cuts[1:]:
        gain = gain * one(*cut)
    return gain


def bell_draw(rng, dims, scale, bound, shards=(), kind=jnp.bfloat16):
    factor_of = block_levels(rng, dims, shards, -0.22, 0.18) if shards else 1.0
    result = jax.random.normal(rng, dims, jnp.float32) * scale * factor_of
    return jnp.minimum(jnp.maximum(result, -bound), bound).astype(kind)


def setup_inputs(seed: int = 0) -> dict:
    seeds = jax.random.split(jax.random.key(seed), 6)
    block_vectors = bell_draw(seeds[0], (NBLK * BS, COLS), 1.0, 6.0, ((0, 512),), jnp.float32)
    hamiltonian = bell_draw(seeds[1], (NBLK, BS, NBR * BS), (NBR * BS) ** -0.5, 0.125, ((0, 512),), jnp.float32)
    pattern = draw_pattern(jax.random.fold_in(seeds[5], 71), 0)
    owned_blocks = draw_owned_blocks(jax.random.fold_in(seeds[5], 71), 0)
    spectrum = jnp.clip(jnp.exp(jax.random.uniform(seeds[4], (2,), jnp.float32, math.log(0.5), math.log(2.0))), 0.5, 2.0)
    return {"block_vectors": block_vectors, "hamiltonian": hamiltonian, "pattern": pattern, "owned_blocks": owned_blocks, "spectrum": spectrum}


def apply_matrix(blocks, hamiltonian, pattern):
    groups = NBLK // RB_CAP
    mats = hamiltonian.reshape(groups, RB_CAP, BS, NBR * BS)
    pats = pattern.reshape(groups, RB_CAP, NBR)

    def one_group(pair):
        mat, pat = pair
        picked = blocks[pat].reshape(RB_CAP, NBR * BS, COLS)
        return jnp.einsum('gik,gkc->gic', mat, picked, precision=lax.Precision.HIGHEST)
    return lax.map(one_group, (mats, pats)).reshape(NBLK, BS, COLS)

def reference(block_vectors, hamiltonian, pattern, owned_blocks, spectrum):
    slots = jnp.arange(NBLK, dtype=jnp.int32)
    live = slots % RB_CAP < jnp.repeat(owned_blocks, RB_CAP)
    live_mask = live.astype(jnp.float32)[:, None, None]
    shift_value = spectrum[0]
    scale_value = spectrum[1]
    first_vec = block_vectors.reshape(NBLK, BS, COLS) * live_mask
    second_vec = live_mask * ((apply_matrix(first_vec, hamiltonian, pattern) - shift_value * first_vec) / scale_value)
    third_vec = live_mask * (2.0 * (apply_matrix(second_vec, hamiltonian, pattern) - shift_value * second_vec) / scale_value - first_vec)
    flat = third_vec.reshape(NBLK * BS, COLS)
    q_mat, r_mat = jnp.linalg.qr(flat)
    signs = jnp.sign(jnp.diagonal(r_mat))
    q_mat = q_mat * signs[None, :]
    r_mat = r_mat * signs[:, None]
    total = jnp.sqrt(jnp.float32(NBLK * BS))
    return (q_mat * total, r_mat / total)
```

```python
import functools

import jax
import jax.numpy as jnp
from jax import lax
from jax.experimental import pallas as pl
from jax.experimental.pallas import tpu as pltpu
from jax.sharding import PartitionSpec as P

BAND = 16
MESH = pl.DeviceIdType.MESH
HIGHEST = lax.Precision.HIGHEST
LANES = 128


def low_lanes(shape):
    return lax.broadcasted_iota(jnp.int32, shape, len(shape) - 1) < shape[-1] // 2


def swap_halves(value):
    return pltpu.roll(value, value.shape[-1] // 2, value.ndim - 1)


def filter_kernel(
    groups, members, blocks, size, neighbours, reach,
    xt_ref, ham_ref, pat_ref, owned_ref, spec_ref,
    y_out, g_out,
    y_buf, xt_buf, h_buf, h_split, v_split, ext_one, ext_two,
    part_buf, scatter_buf, own_buf, reduce_buf, sum_buf, total_buf,
    xt_sem, h_sem, send_one, recv_one, send_two, recv_two, red_sem, round_sem, y_sem,
):
    grp = lax.axis_index("grp")
    dev = lax.axis_index("dev")
    flat = grp * members + dev
    devices = groups * members
    half = blocks // 2
    distances = [d for d in range(-reach, reach + 1) if d]

    def peer(distance):
        other = lax.rem(flat + distance + devices, devices)
        return (lax.div(other, members), lax.rem(other, members))

    def in_groups(step):
        return (lax.rem(grp + step, groups), dev)

    def in_members(step):
        return (grp, lax.rem(dev + step, members))

    x_copy = pltpu.make_async_copy(xt_ref, xt_buf, xt_sem)
    x_copy.start()

    def h_copy(b):
        return pltpu.make_async_copy(ham_ref.at[b], h_buf.at[b], h_sem.at[b])

    for b in range(blocks):
        h_copy(b).start()

    def distinct(offsets, count):
        return sorted({offset % count for offset in offsets} - {0})

    def greet(sem, targets):
        for target in targets:
            pl.semaphore_signal(sem, inc=1, device_id=target, device_id_type=MESH)
        return len(targets)

    def group_ring(offsets):
        return [in_groups(step) for step in distinct(offsets, groups)]

    def member_ring(offsets):
        return [in_members(step) for step in distinct(offsets, members)]

    other_core = dev + 1 - 2 * lax.rem(dev, 2)
    siblings = [
        (grp, lax.rem(other_core + step, members)) for step in [0] + distinct((2, -2), members)
    ]
    barrier = pltpu.get_barrier_semaphore()
    greeted = greet(
        barrier,
        [peer(distance) for distance in distances]
        + siblings
        + member_ring((2, -2))
        + group_ring((1, -1, 4, -4)),
    )
    rounds = [
        member_ring((2, -2)) + group_ring((1, -1, 4, -4)),
        member_ring((4, -4)) + group_ring((4, -4)),
        member_ring((8, -8)),
    ]

    def greet_round(k):
        greet(round_sem.at[k], rounds[k])

    def end_round(k):
        if rounds[k]:
            pl.semaphore_wait(round_sem.at[k], len(rounds[k]))

    owned = owned_ref[0]
    shift = spec_ref[0]
    scale = spec_ref[1]
    low = low_lanes((size, LANES))

    def live(p):
        first = jnp.where(p < owned, 1.0, 0.0).astype(jnp.float32)
        second = jnp.where(p + half < owned, 1.0, 0.0).astype(jnp.float32)
        return jnp.where(low, first, second)

    x_copy.wait()
    for p in range(half):
        both = jnp.concatenate(
            [
                xt_buf[:, p * size : (p + 1) * size],
                xt_buf[:, (p + half) * size : (p + half + 1) * size],
            ],
            axis=0,
        )
        ext_one[reach, p] = live(p) * both.T

    def halo_one(k):
        distance = distances[k]
        return pltpu.make_async_remote_copy(
            src_ref=ext_one.at[reach],
            dst_ref=ext_one.at[reach - distance],
            send_sem=send_one.at[k],
            recv_sem=recv_one.at[k],
            device_id=peer(distance),
            device_id_type=MESH,
        )

    def halo_two(k, p):
        distance = distances[k]
        return pltpu.make_async_remote_copy(
            src_ref=ext_two.at[reach, p],
            dst_ref=ext_two.at[reach - distance, p],
            send_sem=send_two.at[k, p],
            recv_sem=recv_two.at[k, p],
            device_id=peer(distance),
            device_id_type=MESH,
        )

    pl.semaphore_wait(barrier, greeted)
    for k in range(len(distances)):
        halo_one(k).start()
    greet_round(0)

    rows = 16

    @pl.loop(0, blocks)
    def _(b):
        h_copy(b).wait()
        for r in range(0, size, rows):
            value = h_buf[b, r : r + rows, :]
            high = value.astype(jnp.bfloat16)
            h_split[b, r : r + rows, :] = high
            h_split[b, size + r : size + r + rows, :] = (
                value - high.astype(jnp.float32)
            ).astype(jnp.bfloat16)

    def split(ext, slot):
        for p in range(half):
            value = ext[slot, p]
            high = value.astype(jnp.bfloat16).astype(jnp.float32)
            rest = value - high
            v_split[slot * blocks + p] = jnp.where(low, high, swap_halves(rest)).astype(
                jnp.bfloat16
            )
            v_split[slot * blocks + p + half] = jnp.where(
                low, swap_halves(high), rest
            ).astype(jnp.bfloat16)

    start = flat * blocks - reach * blocks
    depth = 4
    last = (2 * reach + 1) * blocks - 1

    def place(b, k):
        return jnp.clip(pat_ref[b, k] - start, 0, last)

    def product(b):
        total = jnp.zeros((2 * size, LANES), jnp.float32)
        for t in range(0, neighbours, depth):
            picked = jnp.concatenate(
                [v_split[place(b, t + q)] for q in range(depth)], axis=0
            )
            total += jnp.dot(
                h_split[b, :, t * size : (t + depth) * size],
                picked,
                preferred_element_type=jnp.float32,
            )
        both = total[:size] + total[size:]
        return both + swap_halves(both)

    def apply_matrix(p):
        return jnp.where(low, product(p), product(p + half))

    split(ext_one, reach)
    for k in range(len(distances)):
        halo_one(k).wait()
        split(ext_one, reach - distances[k])
    end_round(0)
    greet_round(1)

    @pl.loop(0, half)
    def _(p):
        first = ext_one[reach, p]
        ext_two[reach, p] = live(p) * ((apply_matrix(p) - shift * first) / scale)
        for k in range(len(distances)):
            halo_two(k, p).start()

    end_round(1)
    greet_round(2)
    split(ext_two, reach)
    for k in range(len(distances)):
        for p in range(half):
            halo_two(k, p).wait()
        split(ext_two, reach - distances[k])

    @pl.loop(0, half)
    def _(p):
        second = ext_two[reach, p]
        y_buf[p] = live(p) * (
            2.0 * (apply_matrix(p) - shift * second) / scale - ext_one[reach, p]
        )

    y_copy = pltpu.make_async_copy(y_buf, y_out, y_sem)
    y_copy.start()
    gram = jnp.zeros((LANES, LANES), jnp.float32)
    for p in range(half):
        value = y_buf[p]
        gram += lax.dot_general(
            value, value, (((0,), (0,)), ((), ())),
            precision=HIGHEST, preferred_element_type=jnp.float32,
        )
    gram = gram[:size] + swap_halves(gram[size:])
    packed = jnp.where(
        low_lanes((size // 2, LANES)), gram[: size // 2], swap_halves(gram[size // 2 :])
    )
    piece = size // 2 // groups
    for m in range(groups):
        part_buf[m] = packed[m * piece : (m + 1) * piece]
    end_round(2)

    def exchange(step, who, source, target, k):
        return pltpu.make_async_remote_copy(
            src_ref=source, dst_ref=target, send_sem=red_sem.at[2 * k],
            recv_sem=red_sem.at[2 * k + 1], device_id=who(step), device_id_type=MESH,
        )

    def finish(buf, count, k):
        for sem in (2 * k, 2 * k + 1):
            pltpu.make_async_copy(
                buf.at[pl.ds(0, count)], buf.at[pl.ds(0, count)], red_sem.at[sem]
            ).wait()

    @pl.loop(1, groups)
    def _(step):
        to = lax.rem(grp + step, groups)
        exchange(step, in_groups, part_buf.at[to], scatter_buf.at[grp], 0).start()

    scatter_buf[grp] = part_buf[grp]
    finish(scatter_buf, groups - 1, 0)
    own_buf[...] = jnp.sum(scatter_buf[...], axis=0)

    @pl.loop(1, members)
    def _(step):
        exchange(step, in_members, own_buf, reduce_buf.at[dev], 1).start()

    reduce_buf[dev] = own_buf[...]
    finish(reduce_buf, members - 1, 1)
    sum_buf[...] = jnp.sum(reduce_buf[...], axis=0)

    @pl.loop(1, groups)
    def _(step):
        exchange(step, in_groups, sum_buf, total_buf.at[grp], 2).start()

    total_buf[grp] = sum_buf[...]
    finish(total_buf, groups - 1, 2)
    for m in range(groups):
        g_out[m * piece : (m + 1) * piece, :] = total_buf[m]
    y_copy.wait()


def factor_kernel(total, g_ref, y_ref, q_out, r_out, y_buf, y_sem):
    half, size, lanes = y_ref.shape
    y_copy = pltpu.make_async_copy(y_ref, y_buf, y_sem)
    y_copy.start()
    packed = g_ref[...]
    work = jnp.concatenate([packed, swap_halves(packed)], axis=0)
    row = lax.broadcasted_iota(jnp.int32, (size, lanes), 0)
    col = lax.broadcasted_iota(jnp.int32, (size, lanes), 1)
    work = jnp.where(col < size, work, jnp.where(col - size == row, 1.0, 0.0))
    for j in range(size - 1):
        lead = work[j : j + 1, :]
        lead = lead * (1.0 / lead[:, j : j + 1])
        factor = jnp.where(row > j, jnp.broadcast_to(work[:, j : j + 1], work.shape), 0.0)
        work = work - factor * lead
    diagonal = jnp.sum(jnp.where(row == col, work, 0.0), axis=1, keepdims=True)
    work = work * (1.0 / jnp.sqrt(diagonal))
    r_out[...] = jnp.where(col >= row, work, 0.0)[:, :size] * (1.0 / total)
    low = col < size
    inverse = jnp.concatenate(
        [jnp.where(low, swap_halves(work), 0.0), jnp.where(low, 0.0, work)], axis=0
    )
    inverse = inverse * total
    y_copy.wait()
    for p in range(half):
        ortho = lax.dot_general(
            inverse, y_buf[p], (((1,), (1,)), ((), ())),
            precision=HIGHEST, preferred_element_type=jnp.float32,
        )
        q_out[:, p * size : (p + 1) * size] = ortho[:size]
        q_out[:, (p + half) * size : (p + half + 1) * size] = ortho[size:]


def on_device(block_vectors, hamiltonian, pattern, owned_blocks, spectrum):
    blocks, neighbours = pattern.shape
    size = hamiltonian.shape[1]
    columns = block_vectors.shape[1]
    groups = lax.axis_size("grp")
    members = lax.axis_size("dev")
    reach = (BAND + blocks - 1) // blocks
    half = blocks // 2
    slots = 2 * reach + 1
    piece = size // 2 // groups
    f32 = jnp.float32
    vmem = pl.BlockSpec(memory_space=pltpu.VMEM)
    smem = pl.BlockSpec(memory_space=pltpu.SMEM)
    hbm = pl.BlockSpec(memory_space=pltpu.HBM)
    dma = pltpu.SemaphoreType.DMA
    filtered, gram = pl.pallas_call(
        functools.partial(filter_kernel, groups, members, blocks, size, neighbours, reach),
        out_shape=(
            jax.ShapeDtypeStruct((half, size, 2 * columns), f32),
            jax.ShapeDtypeStruct((size // 2, 2 * columns), f32),
        ),
        in_specs=[hbm, hbm, smem, smem, smem],
        out_specs=(hbm, vmem),
        scratch_shapes=[
            pltpu.VMEM((half, size, 2 * columns), f32),
            pltpu.VMEM((columns, blocks * size), f32),
            pltpu.VMEM((blocks, size, neighbours * size), f32),
            pltpu.VMEM((blocks, 2 * size, neighbours * size), jnp.bfloat16),
            pltpu.VMEM((slots * blocks, size, 2 * columns), jnp.bfloat16),
            pltpu.VMEM((slots, half, size, 2 * columns), f32),
            pltpu.VMEM((slots, half, size, 2 * columns), f32),
            pltpu.VMEM((groups, piece, 2 * columns), f32),
            pltpu.VMEM((groups, piece, 2 * columns), f32),
            pltpu.VMEM((piece, 2 * columns), f32),
            pltpu.VMEM((members, piece, 2 * columns), f32),
            pltpu.VMEM((piece, 2 * columns), f32),
            pltpu.VMEM((groups, piece, 2 * columns), f32),
            dma,
            dma((blocks,)),
            dma((2 * reach,)),
            dma((2 * reach,)),
            dma((2 * reach, half)),
            dma((2 * reach, half)),
            dma((6,)),
            pltpu.SemaphoreType.REGULAR((3,)),
            dma,
        ],
        compiler_params=pltpu.CompilerParams(
            collective_id=0, has_side_effects=True, vmem_limit_bytes=60 * 2**20
        ),
        name="filter",
    )(block_vectors.T, hamiltonian, pattern, owned_blocks, spectrum)
    total = float(blocks * size * groups * members) ** 0.5
    ortho, upper = pl.pallas_call(
        functools.partial(factor_kernel, total),
        out_shape=(
            jax.ShapeDtypeStruct((columns, blocks * size), f32),
            jax.ShapeDtypeStruct((columns, columns), f32),
        ),
        in_specs=[vmem, hbm],
        out_specs=(vmem, vmem),
        scratch_shapes=[pltpu.VMEM((half, size, 2 * columns), f32), dma],
        compiler_params=pltpu.CompilerParams(vmem_limit_bytes=60 * 2**20),
        name="factor",
    )(gram, filtered)
    return (ortho.T, upper)


def solution(mesh):
    placed = (
        P(("grp", "dev"), None),
        P(("grp", "dev"), None, None),
        P(("grp", "dev"), None),
        P(("grp", "dev")),
        P(),
    )
    return jax.shard_map(
        on_device,
        mesh=mesh,
        in_specs=placed,
        out_specs=(P(("grp", "dev"), None), P()),
        check_vma=False,
    )
```

```python
import functools

import jax
import jax.numpy as jnp
from jax import lax
from jax.experimental import pallas as pl
from jax.experimental.pallas import tpu as pltpu
from jax.sharding import PartitionSpec as P

BAND = 16
MESH = pl.DeviceIdType.MESH
HIGHEST = lax.Precision.HIGHEST
LANES = 128


def low_lanes(shape):
    return lax.broadcasted_iota(jnp.int32, shape, len(shape) - 1) < shape[-1] // 2


def swap_halves(value):
    return pltpu.roll(value, value.shape[-1] // 2, value.ndim - 1)


def halves(value):
    high = value.astype(jnp.bfloat16)
    return high, (value - high.astype(jnp.float32)).astype(jnp.bfloat16)


def filter_kernel(
    groups, members, blocks, size, neighbours, reach,
    xt_ref, ham_ref, pat_in, owned_in, spec_in,
    y_out, g_out,
    y_buf, xt_buf, h_buf, h_split, v_split, ext_one, ext_two,
    part_buf, scatter_buf, own_buf, reduce_buf, sum_buf, total_buf,
    xt_sem, h_sem, sem_one, sem_two, red_sem, round_sem, y_sem,
    pat_ref, owned_ref, spec_ref, small_sem,
):
    grp = lax.axis_index("grp")
    dev = lax.axis_index("dev")
    flat = grp * members + dev
    devices = groups * members
    half = blocks // 2
    distances = [d for d in range(-reach, reach + 1) if d]

    def peer(distance):
        other = lax.rem(flat + distance + devices, devices)
        return (lax.div(other, members), lax.rem(other, members))

    def in_groups(step):
        return (lax.rem(grp + step, groups), dev)

    def in_members(step):
        return (grp, lax.rem(dev + step, members))

    def distinct(offsets, count):
        return sorted({offset % count for offset in offsets} - {0})

    def greet(sem, targets):
        for target in targets:
            pl.semaphore_signal(sem, inc=1, device_id=target, device_id_type=MESH)
        return len(targets)

    side = 4 if groups % 4 == 0 else groups
    along_x, along_y = lax.div(grp, side), lax.rem(grp, side)

    def plane(offsets_x, offsets_y):
        return [
            (lax.rem(along_x + step, groups // side) * side + along_y, dev)
            for step in distinct(offsets_x, groups // side)
        ] + [
            (along_x * side + lax.rem(along_y + step, side), dev)
            for step in distinct(offsets_y, side)
        ]

    def member_ring(offsets):
        return [in_members(step) for step in distinct(offsets, members)]

    other_core = dev + 1 - 2 * lax.rem(dev, 2)
    siblings = [
        (grp, lax.rem(other_core + step, members)) for step in [0] + distinct((2, -2), members)
    ]
    barrier = pltpu.get_barrier_semaphore()
    greeted = greet(
        barrier,
        siblings + member_ring((2, -2)) + plane((1, -1), (1, -1)),
    )
    for distance in distances:
        inside = (flat + distance >= 0) & (flat + distance < devices)
        greeted = greeted + jnp.where(inside, 1, 0)

        @pl.when(inside)
        def _():
            greet(barrier, [peer(distance)])

    small = [
        pltpu.make_async_copy(source, target, small_sem.at[k])
        for k, (source, target) in enumerate(
            ((owned_in, owned_ref), (spec_in, spec_ref), (pat_in, pat_ref))
        )
    ]
    for copy in small:
        copy.start()
    x_copy = pltpu.make_async_copy(xt_ref, xt_buf, xt_sem)
    x_copy.start()

    def h_copy(b):
        return pltpu.make_async_copy(ham_ref.at[b], h_buf.at[b], h_sem.at[b])

    for b in range(blocks):
        h_copy(b).start()

    rounds = [
        member_ring((2, -2)) + plane((1, -1), (1, -1)),
        member_ring((4, -4)) + plane((2,), (2,)),
        member_ring((8, -8)),
    ]

    def greet_round(k):
        greet(round_sem.at[k], rounds[k])

    def end_round(k):
        if rounds[k]:
            pl.semaphore_wait(round_sem.at[k], len(rounds[k]))

    for copy in small:
        copy.wait()
    owned = owned_ref[0]
    shift = spec_ref[0]
    scale = spec_ref[1]
    low = low_lanes((size, LANES))

    def live(p):
        first = jnp.where(p < owned, 1.0, 0.0).astype(jnp.float32)
        second = jnp.where(p + half < owned, 1.0, 0.0).astype(jnp.float32)
        return jnp.where(low, first, second)

    x_copy.wait()
    for p in range(half):
        both = jnp.concatenate(
            [
                xt_buf[:, p * size : (p + 1) * size],
                xt_buf[:, (p + half) * size : (p + half + 1) * size],
            ],
            axis=0,
        )
        ext_one[reach, p] = live(p) * both.T

    core = lax.rem(dev, 2)
    sibling = (grp, other_core)
    far_slot, near_slot = 4 - 4 * core, 3 - 2 * core
    early = peer(4 * core - 2)
    late = peer(2 - 4 * core)
    below = flat >= 2
    above = flat < devices - 2
    toward = jnp.where(core == 0, below, above)
    away = jnp.where(core == 0, above, below)
    sends = (toward, away, None, away)
    receives = (away, toward, None, toward)

    def given(condition, step):
        if condition is None:
            step()
        else:
            pl.when(condition)(step)

    def halo(ext, sems, kind, p):
        source, target, device = (
            (reach, far_slot, early),
            (reach, 4 * core, late),
            (reach, 1 + 2 * core, sibling),
            (far_slot, near_slot, sibling),
        )[kind]
        return pltpu.make_async_remote_copy(
            src_ref=ext.at[source, p],
            dst_ref=ext.at[target, p],
            send_sem=sems.at[0, kind, p],
            recv_sem=sems.at[1, kind, p],
            device_id=device,
            device_id_type=MESH,
        )

    def send(ext, sems, kind, p):
        given(sends[kind], lambda: halo(ext, sems, kind, p).start())

    def arrive(ext, sems, kind):
        def step():
            for p in range(half):
                halo(ext, sems, kind, p).wait_recv()

        given(receives[kind], step)

    def gather(ext, sems):
        @pl.when(away)
        def _():
            for p in range(half):
                halo(ext, sems, 0, p).wait_recv()
                halo(ext, sems, 3, p).start()

        arrive(ext, sems, 2)
        split(ext, 3 - 2 * core)
        split(ext, far_slot)
        arrive(ext, sems, 1)
        split(ext, 4 * core)
        arrive(ext, sems, 3)
        split(ext, 1 + 2 * core)

    def drain(ext, sems):
        for kind in range(4):

            def step():
                for p in range(half):
                    halo(ext, sems, kind, p).wait_send()

            given(sends[kind], step)

    pl.semaphore_wait(barrier, greeted)
    for kind in range(3):
        for p in range(half):
            send(ext_one, sem_one, kind, p)
    greet_round(0)

    rows = 16

    @pl.loop(0, blocks)
    def _(b):
        h_copy(b).wait()
        for r in range(0, size, rows):
            value = h_buf[b, r : r + rows, :]
            high = value.astype(jnp.bfloat16)
            h_split[b, r : r + rows, :] = high
            h_split[b, size + r : size + r + rows, :] = (
                value - high.astype(jnp.float32)
            ).astype(jnp.bfloat16)

    def split(ext, slot):
        for p in range(half):
            value = ext[slot, p]
            high = value.astype(jnp.bfloat16).astype(jnp.float32)
            rest = value - high
            v_split[slot * blocks + p] = jnp.where(low, high, swap_halves(rest)).astype(
                jnp.bfloat16
            )
            v_split[slot * blocks + p + half] = jnp.where(
                low, swap_halves(high), rest
            ).astype(jnp.bfloat16)

    start = flat * blocks - reach * blocks
    depth = 4
    last = (2 * reach + 1) * blocks - 1

    def place(b, k):
        return jnp.clip(pat_ref[b, k] - start, 0, last)

    def product(b):
        total = jnp.zeros((2 * size, LANES), jnp.float32)
        for t in range(0, neighbours, depth):
            picked = jnp.concatenate(
                [v_split[place(b, t + q)] for q in range(depth)], axis=0
            )
            total += jnp.dot(
                h_split[b, :, t * size : (t + depth) * size],
                picked,
                preferred_element_type=jnp.float32,
            )
        both = total[:size] + total[size:]
        return both + swap_halves(both)

    def apply_matrix(p):
        return jnp.where(low, product(p), product(p + half))

    split(ext_one, reach)
    gather(ext_one, sem_one)
    end_round(0)
    greet_round(1)

    for p in range(half):
        first = ext_one[reach, p]
        ext_two[reach, p] = live(p) * ((apply_matrix(p) - shift * first) / scale)
        for kind in range(3):
            send(ext_two, sem_two, kind, p)

    end_round(1)
    greet_round(2)
    split(ext_two, reach)
    gather(ext_two, sem_two)

    for p in range(half):
        second = ext_two[reach, p]
        y_buf[p] = live(p) * (
            2.0 * (apply_matrix(p) - shift * second) / scale - ext_one[reach, p]
        )

    y_copy = pltpu.make_async_copy(y_buf, y_out, y_sem)
    y_copy.start()
    value = y_buf[...].reshape(half * size, LANES)
    high, rest = halves(value)
    high_t, rest_t = halves(value.T)
    gram = jnp.dot(
        high_t, jnp.concatenate([high, rest], axis=1), preferred_element_type=jnp.float32
    )
    gram = gram[:, :LANES] + gram[:, LANES:]
    gram += jnp.dot(rest_t, high, preferred_element_type=jnp.float32)
    gram = gram[:size] + swap_halves(gram[size:])
    packed = jnp.where(
        low_lanes((size // 2, LANES)), gram[: size // 2], swap_halves(gram[size // 2 :])
    )
    piece = size // 2 // groups
    for m in range(groups):
        part_buf[m] = packed[m * piece : (m + 1) * piece]
    end_round(2)

    def exchange(step, who, source, target, k):
        return pltpu.make_async_remote_copy(
            src_ref=source, dst_ref=target, send_sem=red_sem.at[2 * k],
            recv_sem=red_sem.at[2 * k + 1], device_id=who(step), device_id_type=MESH,
        )

    def finish(buf, count, k):
        for sem in (2 * k, 2 * k + 1):
            pltpu.make_async_copy(
                buf.at[pl.ds(0, count)], buf.at[pl.ds(0, count)], red_sem.at[sem]
            ).wait()

    @pl.loop(1, groups)
    def _(step):
        to = lax.rem(grp + step, groups)
        exchange(step, in_groups, part_buf.at[to], scatter_buf.at[grp], 0).start()

    scatter_buf[grp] = part_buf[grp]
    finish(scatter_buf, groups - 1, 0)
    own_buf[...] = jnp.sum(scatter_buf[...], axis=0)

    @pl.loop(1, members)
    def _(step):
        exchange(step, in_members, own_buf, reduce_buf.at[dev], 1).start()

    reduce_buf[dev] = own_buf[...]
    finish(reduce_buf, members - 1, 1)
    sum_buf[...] = jnp.sum(reduce_buf[...], axis=0)

    @pl.loop(1, groups)
    def _(step):
        exchange(step, in_groups, sum_buf, total_buf.at[grp], 2).start()

    total_buf[grp] = sum_buf[...]
    finish(total_buf, groups - 1, 2)
    for m in range(groups):
        g_out[m * piece : (m + 1) * piece, :] = total_buf[m]
    drain(ext_one, sem_one)
    drain(ext_two, sem_two)
    y_copy.wait()


def eliminate(work):
    rows, lanes = work.shape
    tile = 8
    count = rows // tile
    blocks = [work[tile * r : tile * (r + 1)] for r in range(count)]
    sub = lax.broadcasted_iota(jnp.int32, (tile, lanes), 0)

    def spread(value):
        return jnp.broadcast_to(value, (tile, lanes))

    for q in range(count):
        below = range(q, count)
        column = [
            {r: spread(blocks[r][:, tile * q + c : tile * q + c + 1]) for r in below}
            for c in range(tile)
        ]
        lead = [spread(blocks[q][c : c + 1]) for c in range(tile)]
        pivot = [[spread(column[d][q][c : c + 1]) for d in range(tile)] for c in range(tile)]
        factors = []
        scales = []
        for c in range(0, tile, 2):
            first, cross, second = pivot[c][c], pivot[c][c + 1], pivot[c + 1][c + 1]
            inv_first = 1.0 / first
            inv_second = first * (1.0 / (first * second - cross * cross))
            scales += [inv_first, inv_second]
            ratio = cross * inv_first
            one = {r: column[c][r] * inv_first for r in below}
            one[q] = jnp.where(sub > c, one[q], 0.0)
            two = {r: (column[c + 1][r] - one[r] * cross) * inv_second for r in below}
            two[q] = jnp.where(sub > c + 1, two[q], 0.0)
            factors += [one, two]
            lead[c + 1] = lead[c + 1] - ratio * lead[c]
            rest = {e: pivot[c + 1][e] - ratio * pivot[c][e] for e in range(c + 2, tile)}
            for d in range(c + 2, tile):
                left = pivot[c][d] * inv_first
                right = rest[d] * inv_second
                for r in below:
                    column[d][r] = column[d][r] - (one[r] * pivot[c][d] + two[r] * rest[d])
                lead[d] = lead[d] - (left * lead[c] + right * lead[c + 1])
                for e in range(d, tile):
                    pivot[d][e] = pivot[d][e] - (left * pivot[c][e] + right * rest[e])
        for r in below:
            terms = [factors[c][r] * lead[c] for c in range(tile)]
            while len(terms) > 1:
                terms = [x + y for x, y in zip(terms[::2], terms[1::2])]
            blocks[r] = blocks[r] - terms[0]
        scale = scales[0]
        for c in range(1, tile):
            scale = jnp.where(sub == c, scales[c], scale)
        blocks[q] = blocks[q] * jnp.sqrt(scale)
    return jnp.concatenate(blocks, axis=0)


def factor_kernel(total, g_ref, y_ref, q_out, r_out, y_buf, y_sem):
    half, size, lanes = y_ref.shape
    y_copy = pltpu.make_async_copy(y_ref, y_buf, y_sem)
    y_copy.start()
    packed = g_ref[...]
    work = jnp.concatenate([packed, swap_halves(packed)], axis=0)
    row = lax.broadcasted_iota(jnp.int32, (size, lanes), 0)
    col = lax.broadcasted_iota(jnp.int32, (size, lanes), 1)
    work = eliminate(
        jnp.where(col < size, work, jnp.where(col - size == row, 1.0, 0.0))
    )
    r_out[...] = jnp.where(col >= row, work, 0.0)[:, :size] * (1.0 / total)
    low = col < size
    inverse = jnp.concatenate(
        [jnp.where(low, swap_halves(work), 0.0), jnp.where(low, 0.0, work)], axis=0
    )
    inverse = inverse * total
    y_copy.wait()
    ortho = lax.dot_general(
        inverse, y_buf[...].reshape(half * size, lanes), (((1,), (1,)), ((), ())),
        precision=HIGHEST, preferred_element_type=jnp.float32,
    )
    q_out[:, : half * size] = ortho[:size]
    q_out[:, half * size :] = ortho[size:]


def on_device(block_vectors, hamiltonian, pattern, owned_blocks, spectrum):
    blocks, neighbours = pattern.shape
    size = hamiltonian.shape[1]
    columns = block_vectors.shape[1]
    groups = lax.axis_size("grp")
    members = lax.axis_size("dev")
    reach = (BAND + blocks - 1) // blocks
    half = blocks // 2
    slots = 2 * reach + 1
    piece = size // 2 // groups
    f32 = jnp.float32
    vmem = pl.BlockSpec(memory_space=pltpu.VMEM)
    hbm = pl.BlockSpec(memory_space=pltpu.HBM)
    dma = pltpu.SemaphoreType.DMA
    filtered, gram = pl.pallas_call(
        functools.partial(filter_kernel, groups, members, blocks, size, neighbours, reach),
        out_shape=(
            jax.ShapeDtypeStruct((half, size, 2 * columns), f32),
            jax.ShapeDtypeStruct((size // 2, 2 * columns), f32),
        ),
        in_specs=[hbm] * 5,
        out_specs=(hbm, vmem),
        scratch_shapes=[
            pltpu.VMEM((half, size, 2 * columns), f32),
            pltpu.VMEM((columns, blocks * size), f32),
            pltpu.VMEM((blocks, size, neighbours * size), f32),
            pltpu.VMEM((blocks, 2 * size, neighbours * size), jnp.bfloat16),
            pltpu.VMEM((slots * blocks, size, 2 * columns), jnp.bfloat16),
            pltpu.VMEM((slots, half, size, 2 * columns), f32),
            pltpu.VMEM((slots, half, size, 2 * columns), f32),
            pltpu.VMEM((groups, piece, 2 * columns), f32),
            pltpu.VMEM((groups, piece, 2 * columns), f32),
            pltpu.VMEM((piece, 2 * columns), f32),
            pltpu.VMEM((members, piece, 2 * columns), f32),
            pltpu.VMEM((piece, 2 * columns), f32),
            pltpu.VMEM((groups, piece, 2 * columns), f32),
            dma,
            dma((blocks,)),
            dma((2, 4, half)),
            dma((2, 4, half)),
            dma((6,)),
            pltpu.SemaphoreType.REGULAR((3,)),
            dma,
            pltpu.SMEM((blocks, neighbours), jnp.int32),
            pltpu.SMEM((1,), jnp.int32),
            pltpu.SMEM((2,), f32),
            dma((3,)),
        ],
        compiler_params=pltpu.CompilerParams(
            collective_id=0, has_side_effects=True, vmem_limit_bytes=60 * 2**20
        ),
        name="filter",
    )(block_vectors.T, hamiltonian, pattern, owned_blocks, spectrum)
    total = float(blocks * size * groups * members) ** 0.5
    ortho, upper = pl.pallas_call(
        functools.partial(factor_kernel, total),
        out_shape=(
            jax.ShapeDtypeStruct((columns, blocks * size), f32),
            jax.ShapeDtypeStruct((columns, columns), f32),
        ),
        in_specs=[vmem, hbm],
        out_specs=(vmem, vmem),
        scratch_shapes=[pltpu.VMEM((half, size, 2 * columns), f32), dma],
        compiler_params=pltpu.CompilerParams(vmem_limit_bytes=60 * 2**20),
        name="factor",
    )(gram, filtered)
    return (ortho.T, upper)


def solution(mesh):
    placed = (
        P(("grp", "dev"), None),
        P(("grp", "dev"), None, None),
        P(("grp", "dev"), None),
        P(("grp", "dev")),
        P(),
    )
    return jax.shard_map(
        on_device,
        mesh=mesh,
        in_specs=placed,
        out_specs=(P(("grp", "dev"), None), P()),
        check_vma=False,
    )
```

```python
import functools

import jax
import jax.numpy as jnp
from jax import lax
from jax.experimental import pallas as pl
from jax.experimental.pallas import tpu as pltpu
from jax.sharding import PartitionSpec as P

BAND = 16
MESH = pl.DeviceIdType.MESH
HIGHEST = lax.Precision.HIGHEST
LANES = 128


def low_lanes(shape):
    return lax.broadcasted_iota(jnp.int32, shape, len(shape) - 1) < shape[-1] // 2


def swap_halves(value):
    return pltpu.roll(value, value.shape[-1] // 2, value.ndim - 1)


def filter_kernel(
    groups, members, blocks, size, neighbours, reach,
    xt_ref, ham_ref, pat_in, owned_in, spec_in,
    y_out, g_out,
    y_buf, xt_buf, h_buf, h_split, v_split, ext_one, ext_two,
    part_buf, scatter_buf, own_buf, reduce_buf, sum_buf, total_buf,
    xt_sem, h_sem, sem_one, sem_two, red_sem, round_sem, y_sem,
    pat_ref, owned_ref, spec_ref, small_sem,
):
    grp = lax.axis_index("grp")
    dev = lax.axis_index("dev")
    flat = grp * members + dev
    devices = groups * members
    half = blocks // 2
    distances = [d for d in range(-reach, reach + 1) if d]

    def peer(distance):
        other = lax.rem(flat + distance + devices, devices)
        return (lax.div(other, members), lax.rem(other, members))

    def in_members(step):
        return (grp, lax.rem(dev + step, members))

    x_copy = pltpu.make_async_copy(xt_ref, xt_buf, xt_sem)
    x_copy.start()
    small = [
        pltpu.make_async_copy(source, target, small_sem.at[k])
        for k, (source, target) in enumerate(
            ((owned_in, owned_ref), (spec_in, spec_ref), (pat_in, pat_ref))
        )
    ]
    for copy in small:
        copy.start()

    def distinct(offsets, count):
        return sorted({offset % count for offset in offsets} - {0})

    def greet(sem, targets):
        for target in targets:
            pl.semaphore_signal(sem, inc=1, device_id=target, device_id_type=MESH)
        return len(targets)

    side = 4 if groups % 4 == 0 else groups
    along_x, along_y = lax.div(grp, side), lax.rem(grp, side)

    def plane(offsets_x, offsets_y):
        return [
            (lax.rem(along_x + step, groups // side) * side + along_y, dev)
            for step in distinct(offsets_x, groups // side)
        ] + [
            (along_x * side + lax.rem(along_y + step, side), dev)
            for step in distinct(offsets_y, side)
        ]

    def member_ring(offsets):
        return [in_members(step) for step in distinct(offsets, members)]

    other_core = dev + 1 - 2 * lax.rem(dev, 2)
    siblings = [
        (grp, lax.rem(other_core + step, members)) for step in [0] + distinct((2, -2), members)
    ]
    barrier = pltpu.get_barrier_semaphore()
    greeted = greet(
        barrier,
        siblings + member_ring((2, -2)) + plane((1, -1), (1, -1)),
    )
    for distance in distances:
        inside = (flat + distance >= 0) & (flat + distance < devices)
        greeted = greeted + jnp.where(inside, 1, 0)

        @pl.when(inside)
        def _():
            greet(barrier, [peer(distance)])

    def h_copy(b):
        return pltpu.make_async_copy(ham_ref.at[b], h_buf.at[b], h_sem.at[b])

    for b in range(blocks):
        h_copy(b).start()

    rounds = [
        member_ring((2, -2)) + plane((1, -1), (1, -1)),
        member_ring((4, -4)) + plane((2,), (2,)),
        member_ring((8, -8)),
    ]

    def greet_round(k):
        greet(round_sem.at[k], rounds[k])

    def end_round(k):
        if rounds[k]:
            pl.semaphore_wait(round_sem.at[k], len(rounds[k]))

    for copy in small:
        copy.wait()
    owned = owned_ref[0]
    shift = spec_ref[0]
    scale = spec_ref[1]
    low = low_lanes((size, LANES))

    def live(p):
        first = jnp.where(p < owned, 1.0, 0.0).astype(jnp.float32)
        second = jnp.where(p + half < owned, 1.0, 0.0).astype(jnp.float32)
        return jnp.where(low, first, second)

    x_copy.wait()
    for p in range(half):
        both = jnp.concatenate(
            [
                xt_buf[:, p * size : (p + 1) * size],
                xt_buf[:, (p + half) * size : (p + half + 1) * size],
            ],
            axis=0,
        )
        ext_one[reach, p] = live(p) * both.T

    core = lax.rem(dev, 2)
    sibling = (grp, other_core)
    far_slot, near_slot = 4 - 4 * core, 3 - 2 * core
    early = peer(4 * core - 2)
    late = peer(2 - 4 * core)
    below = flat >= 2
    above = flat < devices - 2
    toward = jnp.where(core == 0, below, above)
    away = jnp.where(core == 0, above, below)
    sends = (toward, away, None, away)
    receives = (away, toward, None, toward)

    def given(condition, step):
        if condition is None:
            step()
        else:
            pl.when(condition)(step)

    def halo(ext, sems, kind, p):
        source, target, device = (
            (reach, far_slot, early),
            (reach, 4 * core, late),
            (reach, 1 + 2 * core, sibling),
            (far_slot, near_slot, sibling),
        )[kind]
        return pltpu.make_async_remote_copy(
            src_ref=ext.at[source, p],
            dst_ref=ext.at[target, p],
            send_sem=sems.at[0, kind, p],
            recv_sem=sems.at[1, kind, p],
            device_id=device,
            device_id_type=MESH,
        )

    def send(ext, sems, kind, p):
        given(sends[kind], lambda: halo(ext, sems, kind, p).start())

    def arrive(ext, sems, kind):
        def step():
            for p in range(half):
                halo(ext, sems, kind, p).wait_recv()

        given(receives[kind], step)

    def gather(ext, sems):
        @pl.when(away)
        def _():
            for p in range(half):
                halo(ext, sems, 0, p).wait_recv()
                halo(ext, sems, 3, p).start()

        arrive(ext, sems, 2)
        split(ext, 3 - 2 * core)
        split(ext, far_slot)
        arrive(ext, sems, 1)
        split(ext, 4 * core)
        arrive(ext, sems, 3)
        split(ext, 1 + 2 * core)

    def drain(ext, sems):
        for kind in range(4):

            def step():
                for p in range(half):
                    halo(ext, sems, kind, p).wait_send()

            given(sends[kind], step)

    pl.semaphore_wait(barrier, greeted)
    for kind in (0, 2, 1):
        for p in range(half):
            send(ext_one, sem_one, kind, p)
    greet_round(0)

    rows = 16

    @pl.loop(0, blocks)
    def _(b):
        h_copy(b).wait()
        for r in range(0, size, rows):
            value = h_buf[b, r : r + rows, :]
            high = value.astype(jnp.bfloat16)
            h_split[b, r : r + rows, :] = high
            h_split[b, size + r : size + r + rows, :] = (
                value - high.astype(jnp.float32)
            ).astype(jnp.bfloat16)

    def split(ext, slot):
        for p in range(half):
            value = ext[slot, p]
            high = value.astype(jnp.bfloat16).astype(jnp.float32)
            rest = value - high
            v_split[slot * blocks + p] = jnp.where(low, high, swap_halves(rest)).astype(
                jnp.bfloat16
            )
            v_split[slot * blocks + p + half] = jnp.where(
                low, swap_halves(high), rest
            ).astype(jnp.bfloat16)

    start = flat * blocks - reach * blocks
    depth = 4
    last = (2 * reach + 1) * blocks - 1

    def place(b, k):
        return jnp.clip(pat_ref[b, k] - start, 0, last)

    def product(b):
        total = jnp.zeros((2 * size, LANES), jnp.float32)
        for t in range(0, neighbours, depth):
            picked = jnp.concatenate(
                [v_split[place(b, t + q)] for q in range(depth)], axis=0
            )
            total += jnp.dot(
                h_split[b, :, t * size : (t + depth) * size],
                picked,
                preferred_element_type=jnp.float32,
            )
        both = total[:size] + total[size:]
        return both + swap_halves(both)

    def apply_matrix(p):
        return jnp.where(low, product(p), product(p + half))

    split(ext_one, reach)
    gather(ext_one, sem_one)
    end_round(0)
    greet_round(1)

    for p in range(half):
        first = ext_one[reach, p]
        ext_two[reach, p] = live(p) * ((apply_matrix(p) - shift * first) / scale)
        for kind in (0, 2):
            send(ext_two, sem_two, kind, p)
    for p in range(half):
        send(ext_two, sem_two, 1, p)

    end_round(1)
    greet_round(2)
    split(ext_two, reach)
    gather(ext_two, sem_two)

    for p in range(half):
        second = ext_two[reach, p]
        y_buf[p] = live(p) * (
            2.0 * (apply_matrix(p) - shift * second) / scale - ext_one[reach, p]
        )

    y_copy = pltpu.make_async_copy(y_buf, y_out, y_sem)
    y_copy.start()
    value = y_buf[...].reshape(half * size, LANES)
    gram = lax.dot_general(
        value, value, (((0,), (0,)), ((), ())),
        precision=HIGHEST, preferred_element_type=jnp.float32,
    )
    gram = gram[:size] + swap_halves(gram[size:])
    packed = jnp.where(
        low_lanes((size // 2, LANES)), gram[: size // 2], swap_halves(gram[size // 2 :])
    )
    piece = size // 2 // groups
    for m in range(groups):
        part_buf[m] = packed[m * piece : (m + 1) * piece]
    end_round(2)

    def in_plane(step):
        return (
            lax.rem(along_x + step[0], groups // side) * side
            + lax.rem(along_y + step[1], side),
            dev,
        )

    def hops(step):
        return sum(min(o, n - o) for o, n in zip(step, (groups // side, side)))

    every = [(x, y) for x in range(groups // side) for y in range(side)]
    far_groups = sorted(every, key=hops)[:0:-1]
    far_members = sorted(range(1, members), key=lambda step: abs(2 * step - members))

    def exchange(device, source, target, k):
        return pltpu.make_async_remote_copy(
            src_ref=source, dst_ref=target, send_sem=red_sem.at[2 * k],
            recv_sem=red_sem.at[2 * k + 1], device_id=device, device_id_type=MESH,
        )

    def finish(buf, count, k):
        for sem in (2 * k, 2 * k + 1):
            pltpu.make_async_copy(
                buf.at[pl.ds(0, count)], buf.at[pl.ds(0, count)], red_sem.at[sem]
            ).wait()

    for step in far_groups:
        exchange(in_plane(step), part_buf.at[in_plane(step)[0]], scatter_buf.at[grp], 0).start()

    scatter_buf[grp] = part_buf[grp]
    finish(scatter_buf, groups - 1, 0)
    own_buf[...] = jnp.sum(scatter_buf[...], axis=0)

    for step in far_members:
        exchange(in_members(step), own_buf, reduce_buf.at[dev], 1).start()

    reduce_buf[dev] = own_buf[...]
    finish(reduce_buf, members - 1, 1)
    sum_buf[...] = jnp.sum(reduce_buf[...], axis=0)

    for step in far_groups:
        exchange(in_plane(step), sum_buf, total_buf.at[grp], 2).start()

    total_buf[grp] = sum_buf[...]
    finish(total_buf, groups - 1, 2)
    for m in range(groups):
        g_out[m * piece : (m + 1) * piece, :] = total_buf[m]
    drain(ext_one, sem_one)
    drain(ext_two, sem_two)
    y_copy.wait()


def eliminate(work):
    rows, lanes = work.shape
    tile = 8
    count = rows // tile
    blocks = [work[tile * r : tile * (r + 1)] for r in range(count)]
    sub = lax.broadcasted_iota(jnp.int32, (tile, lanes), 0)

    def spread(value):
        return jnp.broadcast_to(value, (tile, lanes))

    for q in range(count):
        below = range(q, count)
        column = [
            {r: spread(blocks[r][:, tile * q + c : tile * q + c + 1]) for r in below}
            for c in range(tile)
        ]
        lead = [spread(blocks[q][c : c + 1]) for c in range(tile)]
        pivot = [[spread(column[d][q][c : c + 1]) for d in range(tile)] for c in range(tile)]
        factors = []
        scales = []
        for c in range(0, tile, 2):
            first, cross, second = pivot[c][c], pivot[c][c + 1], pivot[c + 1][c + 1]
            inv_first = 1.0 / first
            inv_second = first * (1.0 / (first * second - cross * cross))
            scales += [inv_first, inv_second]
            ratio = cross * inv_first
            one = {r: column[c][r] * inv_first for r in below}
            one[q] = jnp.where(sub > c, one[q], 0.0)
            two = {r: (column[c + 1][r] - one[r] * cross) * inv_second for r in below}
            two[q] = jnp.where(sub > c + 1, two[q], 0.0)
            factors += [one, two]
            lead[c + 1] = lead[c + 1] - ratio * lead[c]
            rest = {e: pivot[c + 1][e] - ratio * pivot[c][e] for e in range(c + 2, tile)}
            for d in range(c + 2, tile):
                left = pivot[c][d] * inv_first
                right = rest[d] * inv_second
                for r in below:
                    column[d][r] = column[d][r] - (one[r] * pivot[c][d] + two[r] * rest[d])
                lead[d] = lead[d] - (left * lead[c] + right * lead[c + 1])
                for e in range(d, tile):
                    pivot[d][e] = pivot[d][e] - (left * pivot[c][e] + right * rest[e])
        for r in below:
            terms = [factors[c][r] * lead[c] for c in range(tile)]
            while len(terms) > 1:
                terms = [x + y for x, y in zip(terms[::2], terms[1::2])]
            blocks[r] = blocks[r] - terms[0]
        scale = scales[0]
        for c in range(1, tile):
            scale = jnp.where(sub == c, scales[c], scale)
        blocks[q] = blocks[q] * jnp.sqrt(scale)
    return jnp.concatenate(blocks, axis=0)


def factor_kernel(total, g_ref, y_ref, q_out, r_out, y_buf, y_sem):
    half, size, lanes = y_ref.shape
    y_copy = pltpu.make_async_copy(y_ref, y_buf, y_sem)
    y_copy.start()
    packed = g_ref[...]
    work = jnp.concatenate([packed, swap_halves(packed)], axis=0)
    row = lax.broadcasted_iota(jnp.int32, (size, lanes), 0)
    col = lax.broadcasted_iota(jnp.int32, (size, lanes), 1)
    work = eliminate(
        jnp.where(col < size, work, jnp.where(col - size == row, 1.0, 0.0))
    )
    r_out[...] = jnp.where(col >= row, work, 0.0)[:, :size] * (1.0 / total)
    low = col < size
    inverse = jnp.concatenate(
        [jnp.where(low, swap_halves(work), 0.0), jnp.where(low, 0.0, work)], axis=0
    )
    inverse = inverse * total
    y_copy.wait()
    ortho = lax.dot_general(
        inverse, y_buf[...].reshape(half * size, lanes), (((1,), (1,)), ((), ())),
        precision=HIGHEST, preferred_element_type=jnp.float32,
    )
    q_out[:, : half * size] = ortho[:size]
    q_out[:, half * size :] = ortho[size:]


def on_device(block_vectors, hamiltonian, pattern, owned_blocks, spectrum):
    blocks, neighbours = pattern.shape
    size = hamiltonian.shape[1]
    columns = block_vectors.shape[1]
    groups = lax.axis_size("grp")
    members = lax.axis_size("dev")
    reach = (BAND + blocks - 1) // blocks
    half = blocks // 2
    slots = 2 * reach + 1
    piece = size // 2 // groups
    f32 = jnp.float32
    vmem = pl.BlockSpec(memory_space=pltpu.VMEM)
    hbm = pl.BlockSpec(memory_space=pltpu.HBM)
    dma = pltpu.SemaphoreType.DMA
    filtered, gram = pl.pallas_call(
        functools.partial(filter_kernel, groups, members, blocks, size, neighbours, reach),
        out_shape=(
            jax.ShapeDtypeStruct((half, size, 2 * columns), f32),
            jax.ShapeDtypeStruct((size // 2, 2 * columns), f32),
        ),
        in_specs=[hbm] * 5,
        out_specs=(hbm, vmem),
        scratch_shapes=[
            pltpu.VMEM((half, size, 2 * columns), f32),
            pltpu.VMEM((columns, blocks * size), f32),
            pltpu.VMEM((blocks, size, neighbours * size), f32),
            pltpu.VMEM((blocks, 2 * size, neighbours * size), jnp.bfloat16),
            pltpu.VMEM((slots * blocks, size, 2 * columns), jnp.bfloat16),
            pltpu.VMEM((slots, half, size, 2 * columns), f32),
            pltpu.VMEM((slots, half, size, 2 * columns), f32),
            pltpu.VMEM((groups, piece, 2 * columns), f32),
            pltpu.VMEM((groups, piece, 2 * columns), f32),
            pltpu.VMEM((piece, 2 * columns), f32),
            pltpu.VMEM((members, piece, 2 * columns), f32),
            pltpu.VMEM((piece, 2 * columns), f32),
            pltpu.VMEM((groups, piece, 2 * columns), f32),
            dma,
            dma((blocks,)),
            dma((2, 4, half)),
            dma((2, 4, half)),
            dma((6,)),
            pltpu.SemaphoreType.REGULAR((3,)),
            dma,
            pltpu.SMEM((blocks, neighbours), jnp.int32),
            pltpu.SMEM((1,), jnp.int32),
            pltpu.SMEM((2,), f32),
            dma((3,)),
        ],
        compiler_params=pltpu.CompilerParams(
            collective_id=0, has_side_effects=True, vmem_limit_bytes=60 * 2**20
        ),
        name="filter",
    )(block_vectors.T, hamiltonian, pattern, owned_blocks, spectrum)
    total = float(blocks * size * groups * members) ** 0.5
    ortho, upper = pl.pallas_call(
        functools.partial(factor_kernel, total),
        out_shape=(
            jax.ShapeDtypeStruct((columns, blocks * size), f32),
            jax.ShapeDtypeStruct((columns, columns), f32),
        ),
        in_specs=[vmem, hbm],
        out_specs=(vmem, vmem),
        scratch_shapes=[pltpu.VMEM((half, size, 2 * columns), f32), dma],
        compiler_params=pltpu.CompilerParams(vmem_limit_bytes=60 * 2**20),
        name="factor",
    )(gram, filtered)
    return (ortho.T, upper)


def solution(mesh):
    placed = (
        P(("grp", "dev"), None),
        P(("grp", "dev"), None, None),
        P(("grp", "dev"), None),
        P(("grp", "dev")),
        P(),
    )
    return jax.shard_map(
        on_device,
        mesh=mesh,
        in_specs=placed,
        out_specs=(P(("grp", "dev"), None), P()),
        check_vma=False,
    )
```
